256 devices in a mesh: section: 8 (over x, y_hi), example: 32 (over y_lo, z, core).
Axes of the slice: x: 4, y: 4 (y_hi: 2, y_lo: 2; y = y_hi * 2 + y_lo), z: 8, core: 2. Of those that a mesh axis runs over, the one named last changes fastest.
Arguments:
- train_acts: bfloat16 [16384, 28672], P('example', 'section'), may hold values from -6 to 6
- train_grads: bfloat16 [16384, 8192], P('example', 'section'), may hold values from -6 to 6
- act_basis: bfloat16 [28672, 28672], P('section', 'example'), may hold values from -0.0625 to 0.0625
- grad_basis: bfloat16 [8192, 8192], P('section', 'example'), may hold values from -0.125 to 0.125
- query_act: bfloat16 [28672, 512], P('example'), may hold values from -0.03125 to 0.03125
- query_grad: bfloat16 [8192, 512], P('example'), may hold values from -0.0625 to 0.0625
- lengths: int32 [32], P('example'), may hold values from 64 to 512
Outputs:
- scores: float32 [32, 16], P('example')
The draws below stay inside these ranges and needn't reach their ends.
All inputs are finite; a program needn't handle non-finite values.
Results may differ from the reference program's by a relative error of at most 0.0041.
Values may be sent and summed in bfloat16 or wider, within the bound.
No kernel may reach another device: no remote copies, remote signals or barrier semaphores. Data moves between devices by JAX's collectives and lax.ppermute only.
A program may use at most 64 MiB of HBM per device.

```python
import jax
import jax.numpy as jnp

D = 8192
FF = 28672
RANK = 32
SEQ = 512
QUERIES = 16
TRAIN_SEQS = 32
TOKENS = 16384


def touch_ends(entries, own_key, low, high):
    longest = entries.shape.index(max(entries.shape))
    spots = []
    for shift in (0, 1):
        where = [jax.random.randint(jax.random.fold_in(own_key, axis), (), 0, length) for axis, length in enumerate(entries.shape)]
        where[longest] = (where[longest] + shift) % entries.shape[longest]
        spots.append(tuple(where))
    return entries.at[spots[0]].set(low).at[spots[1]].set(high)


def spiked(values, key, source, target, parts, factor):
    def block_of(dim):
        return (jnp.arange(values.shape[dim]) // (values.shape[dim] // parts)).reshape((-1,) + (1,) * (values.ndim - 1 - dim))

    one_side = jax.random.permutation(key, parts)[block_of(target)]
    second = (block_of(target) + parts // 2) % parts
    return jnp.where((block_of(source) == one_side) | (block_of(source) == second), factor * values, values)


def levels(rng, shape, split, smallest, top_value):
    factor_of, own = 1.0, jax.random.fold_in(rng, 6)
    for axis_at, blocks in split:
        draws = jnp.exp(jax.random.uniform(jax.random.fold_in(own, axis_at), (blocks,), jnp.float32, smallest / len(split), top_value / len(split)))
        factor_of = factor_of * jnp.repeat(draws, shape[axis_at] // blocks).reshape([-1 if axis == axis_at else 1 for axis in range(len(shape))])
    return factor_of


def gaussian(own_key, shape, scale, limit, cuts=(), kind=jnp.bfloat16):
    array = scale * jax.random.normal(own_key, shape, jnp.float32)
    if cuts:
        array = array * levels(own_key, shape, cuts, -0.22, 0.18)
    return jnp.clip(array, -limit, limit).astype(kind)


def heavy_noise(own_key, extent, spread, most, shards, heavy, kind=jnp.bfloat16):
    values = spread * jax.random.normal(own_key, extent, jnp.float32)
    if shards:
        values = values * levels(own_key, extent, shards, -0.22, 0.18)
    return jnp.clip(spiked(values, jax.random.fold_in(own_key, 3), *heavy), -most, most).astype(kind)


def setup_inputs(seed: int = 0) -> dict:
    key_list = jax.random.split(jax.random.key(seed), 8)
    train_acts = gaussian(key_list[0], (TOKENS, FF), 1.0, 6.0, ((0, 32), (1, 8)))
    train_grads = gaussian(key_list[1], (TOKENS, D), 1.0, 6.0, ((0, 32), (1, 8)))
    act_basis = heavy_noise(key_list[2], (FF, FF), FF ** -0.5, 0.0625, ((0, 8), (1, 32)), (1, 0, 32, 2.75))
    grad_basis = heavy_noise(key_list[3], (D, D), D ** -0.5, 0.125, ((0, 8), (1, 32)), (1, 0, 32, 2.75))
    query_act = gaussian(key_list[4], (FF, QUERIES * RANK), FF ** -0.5, 0.03125, ((0, 32),))
    query_grad = gaussian(key_list[5], (D, QUERIES * RANK), D ** -0.5, 0.0625, ((0, 32),))
    lengths = touch_ends(jax.random.randint(key_list[6], (TRAIN_SEQS,), SEQ // 8, SEQ + 1), jax.random.fold_in(key_list[6], 1), SEQ // 8, SEQ).astype(jnp.int32)
    return {"train_acts": train_acts, "train_grads": train_grads, "act_basis": act_basis, "grad_basis": grad_basis, "query_act": query_act, "query_grad": query_grad, "lengths": lengths}


def reference(train_acts, train_grads, act_basis, grad_basis, query_act, query_grad, lengths):
    act_factors = jnp.dot(act_basis, query_act, preferred_element_type=jnp.float32).astype(jnp.bfloat16)
    grad_factors = jnp.dot(grad_basis, query_grad, preferred_element_type=jnp.float32).astype(jnp.bfloat16)
    proj_act = jnp.dot(train_acts, act_factors, preferred_element_type=jnp.float32)
    proj_grad = jnp.dot(train_grads, grad_factors, preferred_element_type=jnp.float32)
    product = (proj_act * proj_grad).reshape(TRAIN_SEQS, SEQ, QUERIES, RANK)
    positions = jnp.arange(SEQ, dtype=jnp.int32)
    valid = (positions[None, :] < lengths[:, None]).astype(jnp.float32)
    summed = jnp.sum(product * valid[:, :, None, None], axis=(1, 3))
    return summed * jnp.float32((SEQ * RANK) ** -0.5)
```

```python
import jax
import jax.numpy as jnp
from jax import lax
from jax.sharding import PartitionSpec as P

RANK = 32
SEQ = 512
STREAMS = 2

F32 = jnp.float32
BF16 = jnp.bfloat16


def place(e):
    return e // 16, (e // 2) % 8, e % 2


def example_perm(move):
    pairs = []
    for e in range(32):
        y, z, c = move(*place(e))
        pairs.append((e, (y * 8 + z % 8) * 2 + c))
    return pairs


CORE = example_perm(lambda y, z, c: (y, z, 1 - c))
SIDE = example_perm(lambda y, z, c: (1 - y, z, c))
UP = example_perm(lambda y, z, c: (y, z + 1, c))
DOWN = example_perm(lambda y, z, c: (y, z - 1, c))


def section_perm(move):
    pairs = []
    for s in range(8):
        x, h = move(s // 2, s % 2)
        pairs.append((s, (x % 4) * 2 + h))
    return pairs


def send(value, pairs):
    return lax.ppermute(value, "example", pairs)


def send_section(value, move):
    return lax.ppermute(value, "section", section_perm(move))


def rows(value, index, count):
    return lax.dynamic_slice_in_dim(value, index * count, count, axis=0)


def dot(a, b):
    return jnp.dot(a, b, preferred_element_type=F32)


def local(train_acts, train_grads, act_basis, grad_basis, query_act, query_grad, lengths):
    y, z, c = place(lax.axis_index("example"))
    s = lax.axis_index("section")
    x, h = s // 2, s % 2
    half_a, half_g = act_basis.shape[0] // 2, grad_basis.shape[0] // 2
    part_a, part_g = half_a // 8, half_g // 8
    cols = query_act.shape[1] // STREAMS

    grad_in = send(dot(rows(grad_basis, 1 - c, half_g), query_grad), CORE)
    act_in = send(dot(rows(act_basis, 1 - c, half_a), query_act), CORE)
    grad_own = dot(rows(grad_basis, c, half_g), query_grad)
    act_own = dot(rows(act_basis, c, half_a), query_act)

    acts = [
        lax.dynamic_slice_in_dim(train_acts, k * half_a, half_a, axis=1) for k in (c, 1 - c)
    ]
    grads = [
        lax.dynamic_slice_in_dim(train_grads, k * half_g, half_g, axis=1) for k in (c, 1 - c)
    ]

    def factors(stream):
        span = slice(stream * cols, (stream + 1) * cols)

        def chunk(target):
            target = (target + 8) % 8
            a = rows(act_own, target, part_a) + rows(act_in, target, part_a)
            g = rows(grad_own, target, part_g) + rows(grad_in, target, part_g)
            return jnp.concatenate([a[:, span], g[:, span]], axis=0)

        up = chunk(z + 4)
        down = chunk(z - 3)
        for j in (3, 2, 1):
            up = send(up, UP) + chunk(z + j)
            if j > 1:
                down = send(down, DOWN) + chunk(z - j + 1)
        total = chunk(z) + send(up, UP) + send(down, DOWN)
        a, g = total[:part_a], total[part_a:]

        def side(k):
            return jnp.concatenate([rows(a, k, part_a // 2), rows(g, k, part_g // 2)], axis=0)

        mine = (side(y) + send(side(1 - y), SIDE)).astype(BF16)
        other = send(mine, SIDE)
        low = jnp.where(y == 0, mine, other)
        high = jnp.where(y == 0, other, mine)
        cut = part_a // 2
        whole = jnp.concatenate([low[:cut], high[:cut], low[cut:], high[cut:]], axis=0)
        all_a = jnp.zeros((half_a, cols), BF16)
        all_g = jnp.zeros((half_g, cols), BF16)

        def put(all_a, all_g, value, at):
            at = (at + 8) % 8
            all_a = lax.dynamic_update_slice_in_dim(all_a, value[:part_a], at * part_a, axis=0)
            all_g = lax.dynamic_update_slice_in_dim(all_g, value[part_a:], at * part_g, axis=0)
            return all_a, all_g

        all_a, all_g = put(all_a, all_g, whole, z)
        up = down = whole
        for k in (1, 2, 3, 4):
            up = send(up, UP)
            all_a, all_g = put(all_a, all_g, up, z - k)
            if k < 4:
                down = send(down, DOWN)
                all_a, all_g = put(all_a, all_g, down, z + k)
        return all_a, all_g

    scores = []
    for stream in range(STREAMS):
        all_a, all_g = factors(stream)
        other_a, other_g = send(all_a, CORE), send(all_g, CORE)
        proj_a = dot(acts[0], all_a) + dot(acts[1], other_a)
        proj_g = dot(grads[0], all_g) + dot(grads[1], other_g)
        both = jnp.concatenate([proj_a, proj_g], axis=1)
        quarter = both.shape[0] // 4
        total = rows(both, x, quarter)
        for k in (1, 2, 3):
            piece = rows(both, (x + k) % 4, quarter).astype(BF16)
            total = total + send_section(piece, lambda x, h, k=k: (x + k, h)).astype(F32)
        eighth = quarter // 2
        away = send_section(rows(total, 1 - h, eighth).astype(BF16), lambda x, h: (x, 1 - h))
        total = rows(total, h, eighth) + away.astype(F32)
        token = (x * 2 + h) * eighth + lax.broadcasted_iota(jnp.int32, (eighth, cols), 0)
        product = jnp.where(token < lengths[0], total[:, :cols] * total[:, cols:], 0.0)
        scores.append(jnp.sum(jnp.sum(product, axis=0).reshape(cols // RANK, RANK), axis=1))
    score = jnp.concatenate(scores)[None, :]
    for move in (
        lambda x, h: (x, 1 - h),
        lambda x, h: (x + 1 - 2 * (x % 2), h),
        lambda x, h: (x + 2, h),
    ):
        score = score + send_section(score, move)
    return score * jnp.float32((SEQ * RANK) ** (-0.5))


def solution(mesh):
    in_specs = (
        P("example", "section"),
        P("example", "section"),
        P("section", "example"),
        P("section", "example"),
        P("example", None),
        P("example", None),
        P("example"),
    )
    out_specs = P("example", None)
    return jax.shard_map(local, mesh=mesh, in_specs=in_specs, out_specs=out_specs, check_vma=False)
```

```python
import jax
import jax.numpy as jnp
from jax import lax
from jax.sharding import PartitionSpec as P

RANK = 32
SEQ = 512
STREAMS = 2

F32 = jnp.float32
BF16 = jnp.bfloat16
F16 = jnp.float16


def place(e):
    return e >> 4, (e >> 1) & 7, e & 1


def example_perm(move):
    pairs = []
    for e in range(32):
        y, z, c = move(*place(e))
        pairs.append((e, (y * 8 + z % 8) * 2 + c))
    return pairs


CORE = example_perm(lambda y, z, c: (y, z, 1 - c))
SIDE = example_perm(lambda y, z, c: (1 - y, z, c))
UP = example_perm(lambda y, z, c: (y, z + 1, c))
DOWN = example_perm(lambda y, z, c: (y, z + 7, c))


def section_perm(move):
    pairs = []
    for s in range(8):
        x, h = move(s // 2, s % 2)
        pairs.append((s, (x % 4) * 2 + h))
    return pairs


def send(value, pairs):
    return lax.ppermute(value, "example", pairs)


def send_section(value, move):
    return lax.ppermute(value, "section", section_perm(move))


def rows(value, index, count):
    return lax.dynamic_slice_in_dim(value, index * count, count, axis=0)


def dot(a, b):
    return jnp.dot(a, b, preferred_element_type=F32)


def pack(value):
    top = jnp.max(jnp.abs(value), axis=0, keepdims=True)
    exponent = jnp.clip(jnp.ceil(jnp.log2(top)), -100.0, 100.0)
    scaled = (value * jnp.exp2(14.0 - exponent)).astype(F16)
    return jnp.concatenate([scaled, jnp.repeat(exponent.astype(F16), 16, axis=0)], axis=0)


def unpack(sent):
    return sent[:-16].astype(F32) * jnp.exp2(sent[-16:-15].astype(F32) - 14.0)


def local(train_acts, train_grads, act_basis, grad_basis, query_act, query_grad, lengths):
    y, z, c = place(lax.axis_index("example"))
    s = lax.axis_index("section")
    x, h = s >> 1, s & 1
    half_a, half_g = act_basis.shape[0] // 2, grad_basis.shape[0] // 2
    part_a, part_g = half_a // 8, half_g // 8
    cols = query_act.shape[1] // STREAMS

    grad_in = send(dot(rows(grad_basis, 1 - c, half_g), query_grad), CORE)
    act_in = send(dot(rows(act_basis, 1 - c, half_a), query_act), CORE)
    grad_own = dot(rows(grad_basis, c, half_g), query_grad)
    act_own = dot(rows(act_basis, c, half_a), query_act)
    chunks = []
    for t in range(8):
        at = (z + t) & 7
        a = rows(act_own, at, part_a) + rows(act_in, at, part_a)
        g = rows(grad_own, at, part_g) + rows(grad_in, at, part_g)
        piece = jnp.concatenate([a, g], axis=0)
        chunks.append([piece[:, n * cols : (n + 1) * cols] for n in range(STREAMS)])
    chunks = lax.optimization_barrier(chunks)

    def shift(up, down):
        return send(up, UP), send(down, DOWN)

    def chunk(t, stream):
        return chunks[t & 7][stream]

    long0, long1 = shift(pack(chunk(4, 0)), pack(chunk(-4, 1)))
    ways = [[long0, None], [None, long1]]
    for j in (3, 2, 1):
        for n in range(STREAMS):
            up, down = (chunk(j, n), chunk(-j, n))
            if ways[n][0] is not None:
                up = up + unpack(ways[n][0])
            if ways[n][1] is not None:
                down = down + unpack(ways[n][1])
            ways[n] = shift(pack(up), pack(down))
    totals = [chunk(0, n) + unpack(ways[n][0]) + unpack(ways[n][1]) for n in range(STREAMS)]
    wholes = [(t + unpack(send(pack(t), SIDE))).astype(BF16) for t in totals]

    def put(all_rows, value, at):
        at = at & 7
        all_rows = lax.dynamic_update_slice_in_dim(all_rows, value[:part_a], at * part_a, axis=0)
        return lax.dynamic_update_slice_in_dim(
            all_rows, value[part_a:], half_a + at * part_g, axis=0
        )

    gathered = [put(jnp.zeros((half_a + half_g, cols), BF16), w, z) for w in wholes]
    ways = [(w, w) for w in wholes]
    for k in (1, 2, 3):
        for n in range(STREAMS):
            ways[n] = shift(*ways[n])
            gathered[n] = put(gathered[n], ways[n][0], z - k)
            gathered[n] = put(gathered[n], ways[n][1], z + k)
    last = shift(ways[0][0], ways[1][1])
    gathered = [put(gathered[n], last[n], z + 4) for n in range(STREAMS)]

    acts = [
        lax.dynamic_slice_in_dim(train_acts, k * half_a, half_a, axis=1) for k in (c, 1 - c)
    ]
    grads = [
        lax.dynamic_slice_in_dim(train_grads, k * half_g, half_g, axis=1) for k in (c, 1 - c)
    ]
    scores = []
    for mine in gathered:
        other = send(mine, CORE)
        proj_g = dot(grads[0], mine[half_a:]) + dot(grads[1], other[half_a:])
        proj_a = dot(acts[0], mine[:half_a]) + dot(acts[1], other[:half_a])
        both = jnp.concatenate([proj_a, proj_g], axis=1)
        quarter = both.shape[0] // 4
        total = rows(both, x, quarter)
        for k in (2, 1, 3):
            piece = rows(both, x ^ k, quarter).astype(BF16)
            total = total + send_section(piece, lambda x, h, k=k: (x ^ k, h)).astype(F32)
        eighth = quarter // 2
        away = send_section(rows(total, 1 - h, eighth).astype(BF16), lambda x, h: (x, 1 - h))
        total = rows(total, h, eighth) + away.astype(F32)
        token = s * eighth + lax.broadcasted_iota(jnp.int32, (eighth, cols), 0)
        product = jnp.where(token < lengths[0], total[:, :cols] * total[:, cols:], 0.0)
        scores.append(jnp.sum(jnp.sum(product, axis=0).reshape(cols // RANK, RANK), axis=1))
    score = jnp.concatenate(scores)[None, :]
    for move in (
        lambda x, h: (x, 1 - h),
        lambda x, h: (x ^ 1, h),
        lambda x, h: (x ^ 2, h),
    ):
        score = score + send_section(score, move)
    return score * jnp.float32((SEQ * RANK) ** (-0.5))


def solution(mesh):
    in_specs = (
        P("example", "section"),
        P("example", "section"),
        P("section", "example"),
        P("section", "example"),
        P("example", None),
        P("example", None),
        P("example"),
    )
    out_specs = P("example", None)
    return jax.shard_map(local, mesh=mesh, in_specs=in_specs, out_specs=out_specs, check_vma=False)
```

```python
import jax
import jax.numpy as jnp
from jax import lax
from jax.sharding import PartitionSpec as P

RANK = 32
SEQ = 512
STREAMS = 2

F32 = jnp.float32
BF16 = jnp.bfloat16
F16 = jnp.float16


def place(e):
    return e >> 4, (e >> 1) & 7, e & 1


def example_perm(move):
    pairs = []
    for e in range(32):
        y, z, c = move(*place(e))
        pairs.append((e, (y * 8 + z % 8) * 2 + c))
    return pairs


CORE = example_perm(lambda y, z, c: (y, z, 1 - c))
SIDE = example_perm(lambda y, z, c: (1 - y, z, c))
UP = example_perm(lambda y, z, c: (y, z + 1, c))
DOWN = example_perm(lambda y, z, c: (y, z + 7, c))


def section_perm(move):
    pairs = []
    for s in range(8):
        x, h = move(s // 2, s % 2)
        pairs.append((s, (x % 4) * 2 + h))
    return pairs


def send(value, pairs):
    return lax.ppermute(value, "example", pairs)


def send_section(value, move):
    return lax.ppermute(value, "section", section_perm(move))


def rows(value, index, count):
    return lax.dynamic_slice_in_dim(value, index * count, count, axis=0)


def dot(a, b):
    return jnp.dot(a, b, preferred_element_type=F32)


def pack(value):
    top = jnp.max(jnp.abs(value), axis=0, keepdims=True)
    exponent = jnp.clip(jnp.ceil(jnp.log2(top)), -100.0, 100.0)
    scaled = (value * jnp.exp2(14.0 - exponent)).astype(F16)
    return jnp.concatenate([scaled, jnp.repeat(exponent.astype(F16), 16, axis=0)], axis=0)


def unpack(sent):
    return sent[:-16].astype(F32) * jnp.exp2(sent[-16:-15].astype(F32) - 14.0)


def local(train_acts, train_grads, act_basis, grad_basis, query_act, query_grad, lengths):
    y, z, c = place(lax.axis_index("example"))
    s = lax.axis_index("section")
    x, h = s >> 1, s & 1
    half_a, half_g = act_basis.shape[0] // 2, grad_basis.shape[0] // 2
    part_a, part_g = half_a // 8, half_g // 8
    cols = query_act.shape[1] // STREAMS

    grad_in = send(dot(rows(grad_basis, 1 - c, half_g), query_grad), CORE)
    act_in = send(dot(rows(act_basis, 1 - c, half_a), query_act), CORE)
    grad_own = dot(rows(grad_basis, c, half_g), query_grad)
    act_own = dot(rows(act_basis, c, half_a), query_act)

    def parts(t):
        at = (z + t) & 7
        a = rows(act_own, at, part_a) + rows(act_in, at, part_a)
        g = rows(grad_own, at, part_g) + rows(grad_in, at, part_g)
        piece = jnp.concatenate([a, g], axis=0)
        return [piece[:, n * cols : (n + 1) * cols] for n in range(STREAMS)]

    chunks = {4: lax.optimization_barrier(parts(4))}
    chunks.update(lax.optimization_barrier({t: parts(t) for t in (0, 1, 2, 3, 5, 6, 7)}))

    def shift(up, down):
        return send(up, UP), send(down, DOWN)

    def chunk(t, stream):
        return chunks[t & 7][stream]

    long0, long1 = shift(pack(chunk(4, 0)), pack(chunk(-4, 1)))
    ways = [[long0, None], [None, long1]]
    for j in (3, 2, 1):
        for n in range(STREAMS):
            up, down = (chunk(j, n), chunk(-j, n))
            if ways[n][0] is not None:
                up = up + unpack(ways[n][0])
            if ways[n][1] is not None:
                down = down + unpack(ways[n][1])
            ways[n] = shift(pack(up), pack(down))
    totals = [chunk(0, n) + unpack(ways[n][0]) + unpack(ways[n][1]) for n in range(STREAMS)]
    wholes = [(t + unpack(send(pack(t), SIDE))).astype(BF16) for t in totals]

    def put(gathered, value, at):
        at = at & 7
        a, g = gathered
        a = lax.dynamic_update_slice_in_dim(a, value[:part_a], at * part_a, axis=0)
        return a, lax.dynamic_update_slice_in_dim(g, value[part_a:], at * part_g, axis=0)

    empty = jnp.zeros((half_a, cols), BF16), jnp.zeros((half_g, cols), BF16)
    gathered = [put(empty, w, z) for w in wholes]
    ways = [(w, w) for w in wholes]
    for k in (1, 2, 3):
        for n in range(STREAMS):
            ways[n] = shift(*ways[n])
            gathered[n] = put(gathered[n], ways[n][0], z - k)
            gathered[n] = put(gathered[n], ways[n][1], z + k)
    last = shift(ways[0][0], ways[1][1])
    gathered = [put(gathered[n], last[n], z + 4) for n in range(STREAMS)]

    acts = [
        lax.dynamic_slice_in_dim(train_acts, k * half_a, half_a, axis=1) for k in (c, 1 - c)
    ]
    grads = [
        lax.dynamic_slice_in_dim(train_grads, k * half_g, half_g, axis=1) for k in (c, 1 - c)
    ]
    scores = []
    for mine_a, mine_g in gathered:
        other_a, other_g = send(mine_a, CORE), send(mine_g, CORE)
        proj_g = dot(grads[0], mine_g) + dot(grads[1], other_g)
        proj_a = dot(acts[0], mine_a) + dot(acts[1], other_a)
        both = jnp.concatenate([proj_a, proj_g], axis=1)
        quarter = both.shape[0] // 4
        total = rows(both, x, quarter)
        for k in (2, 1, 3):
            piece = rows(both, x ^ k, quarter).astype(BF16)
            total = total + send_section(piece, lambda x, h, k=k: (x ^ k, h)).astype(F32)
        mine = pack(total)
        total = unpack(mine) + unpack(send_section(mine, lambda x, h: (x, 1 - h)))
        token = x * quarter + lax.broadcasted_iota(jnp.int32, (quarter, cols), 0)
        product = jnp.where(token < lengths[0], total[:, :cols] * total[:, cols:], 0.0)
        scores.append(jnp.sum(jnp.sum(product, axis=0).reshape(cols // RANK, RANK), axis=1))
    score = jnp.concatenate(scores)[None, :]
    table = lax.dynamic_update_slice(jnp.zeros((4, score.shape[1]), F32), score, (x, 0))
    for k in (2, 1, 3):
        got = send_section(score, lambda x, h, k=k: (x ^ k, h))
        table = lax.dynamic_update_slice(table, got, (x ^ k, 0))
    score = (table[0:1] + table[1:2]) + (table[2:3] + table[3:4])
    return score * jnp.float32((SEQ * RANK) ** (-0.5))


def solution(mesh):
    in_specs = (
        P("example", "section"),
        P("example", "section"),
        P("section", "example"),
        P("section", "example"),
        P("example", None),
        P("example", None),
        P("example"),
    )
    out_specs = P("example", None)
    return jax.shard_map(local, mesh=mesh, in_specs=in_specs, out_specs=out_specs, check_vma=False)
```

```python
import jax
import jax.numpy as jnp
from jax import lax
from jax.sharding import PartitionSpec as P

RANK = 32
SEQ = 512
STREAMS = 2

F32 = jnp.float32
BF16 = jnp.bfloat16
F16 = jnp.float16


def place(e):
    return e >> 4, (e >> 1) & 7, e & 1


def example_perm(move):
    pairs = []
    for e in range(32):
        y, z, c = move(*place(e))
        pairs.append((e, (y * 8 + z % 8) * 2 + c))
    return pairs


CORE = example_perm(lambda y, z, c: (y, z, 1 - c))
SIDE = example_perm(lambda y, z, c: (1 - y, z, c))
UP = example_perm(lambda y, z, c: (y, z + 1, c))
DOWN = example_perm(lambda y, z, c: (y, z + 7, c))
TURN = example_perm(lambda y, z, c: (y, z + (7 if c else 1), c))


def section_perm(move):
    pairs = []
    for s in range(8):
        x, h = move(s // 2, s % 2)
        pairs.append((s, (x % 4) * 2 + h))
    return pairs


def send(value, pairs):
    return lax.ppermute(value, "example", pairs)


def send_section(value, move):
    return lax.ppermute(value, "section", section_perm(move))


def rows(value, index, count):
    return lax.dynamic_slice_in_dim(value, index * count, count, axis=0)


def dot(a, b):
    return jnp.dot(a, b, preferred_element_type=F32)


def pack(value):
    top = jnp.max(jnp.abs(value), axis=0, keepdims=True)
    exponent = jnp.clip(jnp.ceil(jnp.log2(top)), -100.0, 100.0)
    scaled = (value * jnp.exp2(14.0 - exponent)).astype(F16)
    return jnp.concatenate([scaled, jnp.repeat(exponent.astype(F16), 16, axis=0)], axis=0)


def unpack(sent):
    return sent[:-16].astype(F32) * jnp.exp2(sent[-16:-15].astype(F32) - 14.0)


def local(train_acts, train_grads, act_basis, grad_basis, query_act, query_grad, lengths):
    y, z, c = place(lax.axis_index("example"))
    s = lax.axis_index("section")
    x, h = s >> 1, s & 1
    half_a, half_g = act_basis.shape[0] // 2, grad_basis.shape[0] // 2
    part_a, part_g = half_a // 8, half_g // 8
    cols = query_act.shape[1] // STREAMS

    grad_in = send(dot(rows(grad_basis, 1 - c, half_g), query_grad), CORE)
    act_in = send(dot(rows(act_basis, 1 - c, half_a), query_act), CORE)
    grad_own = dot(rows(grad_basis, c, half_g), query_grad)
    act_own = dot(rows(act_basis, c, half_a), query_act)

    def parts(t):
        at = (z + t) & 7
        a = rows(act_own, at, part_a) + rows(act_in, at, part_a)
        g = rows(grad_own, at, part_g) + rows(grad_in, at, part_g)
        piece = jnp.concatenate([a, g], axis=0)
        return [piece[:, n * cols : (n + 1) * cols] for n in range(STREAMS)]

    chunks = {4: lax.optimization_barrier(parts(4))}
    chunks.update(lax.optimization_barrier({t: parts(t) for t in (0, 1, 2, 3, 5, 6, 7)}))

    def shift(up, down):
        return send(up, UP), send(down, DOWN)

    def chunk(t, stream):
        return chunks[t & 7][stream]

    long0, long1 = shift(pack(chunk(4, 0)), pack(chunk(-4, 1)))
    ways = [[long0, None], [None, long1]]
    for j in (3, 2, 1):
        for n in range(STREAMS):
            up, down = (chunk(j, n), chunk(-j, n))
            if ways[n][0] is not None:
                up = up + unpack(ways[n][0])
            if ways[n][1] is not None:
                down = down + unpack(ways[n][1])
            ways[n] = shift(pack(up), pack(down))
    totals = [chunk(0, n) + unpack(ways[n][0]) + unpack(ways[n][1]) for n in range(STREAMS)]
    wholes = [(t + unpack(send(pack(t), SIDE))).astype(BF16) for t in totals]

    low = c == 0

    def chip(mine):
        other = send(mine, CORE)
        a, b = jnp.where(low, mine, other), jnp.where(low, other, mine)
        return jnp.concatenate([a[:part_a], b[:part_a], a[part_a:], b[part_a:]], axis=0)

    def put(gathered, value, at):
        a, g = gathered
        at = at & 7
        new_a = value[: 2 * part_a].reshape(2, 1, part_a, cols)
        new_g = value[2 * part_a :].reshape(2, 1, part_g, cols)
        return (
            lax.dynamic_update_slice(a, new_a, (0, at, 0, 0)),
            lax.dynamic_update_slice(g, new_g, (0, at, 0, 0)),
        )

    empty = jnp.zeros((2, 8, part_a, cols), BF16), jnp.zeros((2, 8, part_g, cols), BF16)
    ways = [chip(w) for w in wholes]
    gathered = [put(empty, w, z) for w in ways]
    for k in (1, 2, 3):
        near, far = jnp.where(low, z - k, z + k), jnp.where(low, z + k, z - k)
        for n in range(STREAMS):
            ways[n] = send(ways[n], TURN)
            gathered[n] = put(gathered[n], ways[n], near)
            gathered[n] = put(gathered[n], send(ways[n], CORE), far)
    last = send(jnp.where(low, ways[0], ways[1]), TURN)
    other = send(last, CORE)
    gathered[0] = put(gathered[0], jnp.where(low, last, other), z + 4)
    gathered[1] = put(gathered[1], jnp.where(low, other, last), z + 4)

    scores = []
    for all_a, all_g in gathered:
        proj_g = dot(train_grads, all_g.reshape(2 * half_g, cols))
        proj_a = dot(train_acts, all_a.reshape(2 * half_a, cols))
        both = jnp.concatenate([proj_a, proj_g], axis=1)
        quarter = both.shape[0] // 4
        total = rows(both, x, quarter)
        for k in (2, 1, 3):
            piece = rows(both, x ^ k, quarter).astype(BF16)
            total = total + send_section(piece, lambda x, h, k=k: (x ^ k, h)).astype(F32)
        mine = pack(total)
        total = unpack(mine) + unpack(send_section(mine, lambda x, h: (x, 1 - h)))
        token = x * quarter + lax.broadcasted_iota(jnp.int32, (quarter, cols), 0)
        product = jnp.where(token < lengths[0], total[:, :cols] * total[:, cols:], 0.0)
        scores.append(jnp.sum(jnp.sum(product, axis=0).reshape(cols // RANK, RANK), axis=1))
    score = jnp.concatenate(scores)[None, :]
    table = lax.dynamic_update_slice(jnp.zeros((4, score.shape[1]), F32), score, (x, 0))
    for k in (2, 1, 3):
        got = send_section(score, lambda x, h, k=k: (x ^ k, h))
        table = lax.dynamic_update_slice(table, got, (x ^ k, 0))
    score = (table[0:1] + table[1:2]) + (table[2:3] + table[3:4])
    return score * jnp.float32((SEQ * RANK) ** (-0.5))


def solution(mesh):
    in_specs = (
        P("example", "section"),
        P("example", "section"),
        P("section", "example"),
        P("section", "example"),
        P("example", None),
        P("example", None),
        P("example"),
    )
    out_specs = P("example", None)
    return jax.shard_map(local, mesh=mesh, in_specs=in_specs, out_specs=out_specs, check_vma=False)
```

```python
import jax
import jax.numpy as jnp
from jax import lax
from jax.sharding import PartitionSpec as P

RANK = 32
SEQ = 512
STREAMS = 2

F32 = jnp.float32
BF16 = jnp.bfloat16
F16 = jnp.float16


def place(e):
    return e >> 4, (e >> 1) & 7, e & 1


def example_perm(move):
    pairs = []
    for e in range(32):
        y, z, c = move(*place(e))
        pairs.append((e, (y * 8 + z % 8) * 2 + c))
    return pairs


CORE = example_perm(lambda y, z, c: (y, z, 1 - c))
SIDE = example_perm(lambda y, z, c: (1 - y, z, c))
UP = example_perm(lambda y, z, c: (y, z + (7 if c else 1), c))
DOWN = example_perm(lambda y, z, c: (y, z + (1 if c else 7), c))


def section_perm(move):
    pairs = []
    for s in range(8):
        x, h = move(s // 2, s % 2)
        pairs.append((s, (x % 4) * 2 + h))
    return pairs


def send(value, pairs):
    return lax.ppermute(value, "example", pairs)


def send_section(value, move):
    return lax.ppermute(value, "section", section_perm(move))


def rows(value, index, count):
    return lax.dynamic_slice_in_dim(value, index * count, count, axis=0)


def dot(a, b):
    return jnp.dot(a, b, preferred_element_type=F32)


def pack(value):
    top = jnp.max(jnp.abs(value), axis=0, keepdims=True)
    exponent = jnp.clip(jnp.ceil(jnp.log2(top)), -100.0, 100.0)
    scaled = (value * jnp.exp2(14.0 - exponent)).astype(F16)
    return jnp.concatenate([scaled, jnp.repeat(exponent.astype(F16), 16, axis=0)], axis=0)


def unpack(sent):
    return sent[:-16].astype(F32) * jnp.exp2(sent[-16:-15].astype(F32) - 14.0)


def local(train_acts, train_grads, act_basis, grad_basis, query_act, query_grad, lengths):
    y, z, c = place(lax.axis_index("example"))
    s = lax.axis_index("section")
    x, h = s >> 1, s & 1
    half_a, half_g = act_basis.shape[0] // 2, grad_basis.shape[0] // 2
    part_a, part_g = half_a // 8, half_g // 8
    cols = query_act.shape[1] // STREAMS

    grad_in = send(dot(rows(grad_basis, 1 - c, half_g), query_grad), CORE)
    act_in = send(dot(rows(act_basis, 1 - c, half_a), query_act), CORE)
    grad_own = dot(rows(grad_basis, c, half_g), query_grad)
    act_own = dot(rows(act_basis, c, half_a), query_act)

    sign = 1 - 2 * c

    def parts(t):
        at = (z + sign * t) & 7
        a = rows(act_own, at, part_a) + rows(act_in, at, part_a)
        g = rows(grad_own, at, part_g) + rows(grad_in, at, part_g)
        piece = jnp.concatenate([a, g], axis=0)
        return [piece[:, n * cols : (n + 1) * cols] for n in range(STREAMS)]

    chunks = {4: lax.optimization_barrier(parts(4))}
    chunks.update(lax.optimization_barrier({t: parts(t) for t in (0, 1, 2, 3, 5, 6, 7)}))

    def shift(up, down):
        return send(up, UP), send(down, DOWN)

    def chunk(t, stream):
        return chunks[t & 7][stream]

    long0, long1 = shift(pack(chunk(4, 0)), pack(chunk(-4, 1)))
    ways = [[long0, None], [None, long1]]
    for j in (3, 2, 1):
        for n in range(STREAMS):
            up, down = (chunk(j, n), chunk(-j, n))
            if ways[n][0] is not None:
                up = up + unpack(ways[n][0])
            if ways[n][1] is not None:
                down = down + unpack(ways[n][1])
            ways[n] = shift(pack(up), pack(down))
    totals = [chunk(0, n) + unpack(ways[n][0]) + unpack(ways[n][1]) for n in range(STREAMS)]
    wholes = [(t + unpack(send(pack(t), SIDE))).astype(BF16) for t in totals]

    def put(gathered, value, at):
        at = at & 7
        a, g = gathered
        a = lax.dynamic_update_slice_in_dim(a, value[:part_a], at * part_a, axis=0)
        return a, lax.dynamic_update_slice_in_dim(g, value[part_a:], at * part_g, axis=0)

    empty = jnp.zeros((half_a, cols), BF16), jnp.zeros((half_g, cols), BF16)
    gathered = [put(empty, w, z) for w in wholes]
    ways = [(w, w) for w in wholes]
    for k in (1, 2, 3):
        for n in range(STREAMS):
            ways[n] = shift(*ways[n])
            gathered[n] = put(gathered[n], ways[n][0], z - sign * k)
            gathered[n] = put(gathered[n], ways[n][1], z + sign * k)
    last = shift(ways[0][0], ways[1][1])
    gathered = [put(gathered[n], last[n], z + 4) for n in range(STREAMS)]

    acts = [
        lax.dynamic_slice_in_dim(train_acts, k * half_a, half_a, axis=1) for k in (c, 1 - c)
    ]
    grads = [
        lax.dynamic_slice_in_dim(train_grads, k * half_g, half_g, axis=1) for k in (c, 1 - c)
    ]
    scores = []
    for mine_a, mine_g in gathered:
        other_a, other_g = send(mine_a, CORE), send(mine_g, CORE)
        proj_g = dot(grads[0], mine_g) + dot(grads[1], other_g)
        proj_a = dot(acts[0], mine_a) + dot(acts[1], other_a)
        both = jnp.concatenate([proj_a, proj_g], axis=1)
        quarter = both.shape[0] // 4
        total = rows(both, x, quarter)
        for k in (2, 1, 3):
            piece = rows(both, x ^ k, quarter).astype(BF16)
            total = total + send_section(piece, lambda x, h, k=k: (x ^ k, h)).astype(F32)
        mine = pack(total)
        total = unpack(mine) + unpack(send_section(mine, lambda x, h: (x, 1 - h)))
        token = x * quarter + lax.broadcasted_iota(jnp.int32, (quarter, cols), 0)
        product = jnp.where(token < lengths[0], total[:, :cols] * total[:, cols:], 0.0)
        scores.append(jnp.sum(jnp.sum(product, axis=0).reshape(cols // RANK, RANK), axis=1))
    score = jnp.concatenate(scores)[None, :]
    table = lax.dynamic_update_slice(jnp.zeros((4, score.shape[1]), F32), score, (x, 0))
    for k in (2, 1, 3):
        got = send_section(score, lambda x, h, k=k: (x ^ k, h))
        table = lax.dynamic_update_slice(table, got, (x ^ k, 0))
    score = (table[0:1] + table[1:2]) + (table[2:3] + table[3:4])
    return score * jnp.float32((SEQ * RANK) ** (-0.5))


def solution(mesh):
    in_specs = (
        P("example", "section"),
        P("example", "section"),
        P("section", "example"),
        P("section", "example"),
        P("example", None),
        P("example", None),
        P("example"),
    )
    out_specs = P("example", None)
    return jax.shard_map(local, mesh=mesh, in_specs=in_specs, out_specs=out_specs, check_vma=False)
```

```python
import functools

import jax
import jax.numpy as jnp
from jax import lax
from jax.sharding import PartitionSpec as P

RANK = 32
SEQ = 512
STREAMS = 2

F32 = jnp.float32
BF16 = jnp.bfloat16
F16 = jnp.float16


def place(e):
    return e >> 4, (e >> 1) & 7, e & 1


def example_perm(move):
    pairs = []
    for e in range(32):
        y, z, c = move(*place(e))
        pairs.append((e, (y * 8 + z % 8) * 2 + c))
    return pairs


CORE = example_perm(lambda y, z, c: (y, z, 1 - c))
SIDE = example_perm(lambda y, z, c: (1 - y, z, c))
UP = example_perm(lambda y, z, c: (y, z + 1, c))
DOWN = example_perm(lambda y, z, c: (y, z + 7, c))


def section_perm(move):
    pairs = []
    for s in range(8):
        x, h = move(s // 2, s % 2)
        pairs.append((s, (x % 4) * 2 + h))
    return pairs


def send(value, pairs):
    return lax.ppermute(value, "example", pairs)


def send_section(value, move):
    return lax.ppermute(value, "section", section_perm(move))


def rows(value, index, count):
    return lax.dynamic_slice_in_dim(value, index * count, count, axis=0)


def dot(a, b):
    return jnp.dot(a, b, preferred_element_type=F32)


def exponent_of(value):
    top = jnp.max(jnp.abs(value), axis=0, keepdims=True)
    return jnp.clip(jnp.ceil(jnp.log2(top)), -100.0, 100.0)


def pack(value, exponent):
    scaled = (value * jnp.exp2(14.0 - exponent)).astype(F16)
    return jnp.concatenate([scaled, jnp.repeat(exponent.astype(F16), 16, axis=0)], axis=0)


def unpack(sent):
    exponent = sent[-16:-15].astype(F32)
    return sent[:-16].astype(F32) * jnp.exp2(exponent - 14.0), exponent


def local(train_acts, train_grads, act_basis, grad_basis, query_act, query_grad, lengths):
    y, z, c = place(lax.axis_index("example"))
    s = lax.axis_index("section")
    x, h = s >> 1, s & 1
    half_a, half_g = act_basis.shape[0] // 2, grad_basis.shape[0] // 2
    part_a, part_g = half_a // 8, half_g // 8
    cols = query_act.shape[1] // STREAMS

    grad_in = send(dot(rows(grad_basis, 1 - c, half_g), query_grad), CORE)
    act_in = send(dot(rows(act_basis, 1 - c, half_a), query_act), CORE)
    grad_own = dot(rows(grad_basis, c, half_g), query_grad)
    act_own = dot(rows(act_basis, c, half_a), query_act)

    def parts(t):
        at = (z + t) & 7
        a = rows(act_own, at, part_a) + rows(act_in, at, part_a)
        g = rows(grad_own, at, part_g) + rows(grad_in, at, part_g)
        piece = jnp.concatenate([a, g], axis=0)
        return [piece[:, n * cols : (n + 1) * cols] for n in range(STREAMS)]

    chunks = {4: lax.optimization_barrier(parts(4))}
    chunks.update(lax.optimization_barrier({t: parts(t) for t in (0, 1, 2, 3, 5, 6, 7)}))

    def shift(up, down):
        return send(up, UP), send(down, DOWN)

    def chunk(t, stream):
        return chunks[t & 7][stream]

    bounds = []
    for n in range(STREAMS):
        tops = [jnp.max(jnp.abs(chunk(t, n)), axis=0, keepdims=True) for t in range(8)]
        bound = jnp.ceil(jnp.log2(functools.reduce(jnp.maximum, tops)))
        bounds.append(lax.optimization_barrier([jnp.clip(bound, -100.0, 100.0)] * 8))

    def hop(t, n, sent):
        bound = bounds[n][t & 7]
        if sent is None:
            return pack(chunk(t, n), bound)
        value, exponent = unpack(sent)
        return pack(chunk(t, n) + value, jnp.maximum(exponent, bound) + 1.0)

    long0, long1 = shift(hop(4, 0, None), hop(-4, 1, None))
    ways = [[long0, None], [None, long1]]
    for j in (3, 2, 1):
        for n in range(STREAMS):
            ways[n] = shift(hop(j, n, ways[n][0]), hop(-j, n, ways[n][1]))
    wholes = []
    for n in range(STREAMS):
        (up, up_bound), (down, down_bound) = unpack(ways[n][0]), unpack(ways[n][1])
        total = chunk(0, n) + up + down
        bound = jnp.maximum(jnp.maximum(up_bound, down_bound), bounds[n][0]) + 2.0
        wholes.append((total + unpack(send(pack(total, bound), SIDE))[0]).astype(BF16))

    def put(gathered, value, at):
        at = at & 7
        a, g = gathered
        a = lax.dynamic_update_slice_in_dim(a, value[:part_a], at * part_a, axis=0)
        return a, lax.dynamic_update_slice_in_dim(g, value[part_a:], at * part_g, axis=0)

    empty = jnp.zeros((half_a, cols), BF16), jnp.zeros((half_g, cols), BF16)
    gathered = [put(empty, w, z) for w in wholes]
    ways = [(w, w) for w in wholes]
    for k in (1, 2, 3):
        for n in range(STREAMS):
            ways[n] = shift(*ways[n])
            gathered[n] = put(gathered[n], ways[n][0], z - k)
            gathered[n] = put(gathered[n], ways[n][1], z + k)
    last = shift(ways[0][0], ways[1][1])
    gathered = [put(gathered[n], last[n], z + 4) for n in range(STREAMS)]

    acts = [
        lax.dynamic_slice_in_dim(train_acts, k * half_a, half_a, axis=1) for k in (c, 1 - c)
    ]
    grads = [
        lax.dynamic_slice_in_dim(train_grads, k * half_g, half_g, axis=1) for k in (c, 1 - c)
    ]
    scores = []
    for mine_a, mine_g in gathered:
        other_a, other_g = send(mine_a, CORE), send(mine_g, CORE)
        proj_g = dot(grads[0], mine_g) + dot(grads[1], other_g)
        proj_a = dot(acts[0], mine_a) + dot(acts[1], other_a)
        both = jnp.concatenate([proj_a, proj_g], axis=1)
        quarter = both.shape[0] // 4
        total = rows(both, x, quarter)
        for k in (2, 1, 3):
            piece = rows(both, x ^ k, quarter).astype(BF16)
            total = total + send_section(piece, lambda x, h, k=k: (x ^ k, h)).astype(F32)
        mine = pack(total, exponent_of(total))
        away = send_section(mine, lambda x, h: (x, 1 - h))
        total = unpack(mine)[0] + unpack(away)[0]
        token = x * quarter + lax.broadcasted_iota(jnp.int32, (quarter, cols), 0)
        product = jnp.where(token < lengths[0], total[:, :cols] * total[:, cols:], 0.0)
        scores.append(jnp.sum(jnp.sum(product, axis=0).reshape(cols // RANK, RANK), axis=1))
    score = jnp.concatenate(scores)[None, :]
    table = lax.dynamic_update_slice(jnp.zeros((4, score.shape[1]), F32), score, (x, 0))
    for k in (2, 1, 3):
        got = send_section(score, lambda x, h, k=k: (x ^ k, h))
        table = lax.dynamic_update_slice(table, got, (x ^ k, 0))
    score = (table[0:1] + table[1:2]) + (table[2:3] + table[3:4])
    return score * jnp.float32((SEQ * RANK) ** (-0.5))


def solution(mesh):
    in_specs = (
        P("example", "section"),
        P("example", "section"),
        P("section", "example"),
        P("section", "example"),
        P("example", None),
        P("example", None),
        P("example"),
    )
    out_specs = P("example", None)
    return jax.shard_map(local, mesh=mesh, in_specs=in_specs, out_specs=out_specs, check_vma=False)
```
